32 devices in a mesh: groups: 2 (over y), row: 4 (over z), col: 4 (over x, core).
Axes of the slice: x: 2, y: 2, z: 4, core: 2. Of those that a mesh axis runs over, the one named last changes fastest.
Arguments:
- left_tiles: bfloat16 [4096, 5120], P(('groups', 'row'), 'col'), parts along dimension 0, may hold values from -6 to 6
- right_tiles: bfloat16 [10240, 3072], P(('groups', 'row'), 'col'), parts along dimension 0, may hold values from -0.375 to 0.375
- left_blocks: int32 [8, 4, 10], P(('groups', 'row'), 'col'), parts along dimension 0, may hold values from 0 to 9, each once within a row
- left_count: int32 [8, 4], P(('groups', 'row'), 'col'), parts along dimension 0, may hold values from 0 to 4, as said below
- right_blocks: int32 [8, 4, 15], P(('groups', 'row'), 'col'), parts along dimension 0, may hold values from 0 to 14, each once within a row
- right_count: int32 [8, 4], P(('groups', 'row'), 'col'), parts along dimension 0, may hold values from 0 to 4, as said below
Outputs:
- partial_square: float32 [4096, 3072], P(('groups', 'row'), 'col'), parts along dimension 0
The draws below stay inside these ranges and needn't reach their ends.
There are 2 independent parts, one for each index of `groups`. The reference program is written for one: setup_inputs(seed, part) draws one part's arguments, and reference() takes and returns one part's arrays. A program takes and returns all parts, laid end to end along the dimension named above; each array names one. Nothing has to cross between parts.
Inputs may be any that keep to these rules, and one draw needn't show every extreme that they name: `left_blocks`: each tile's entries name every block number of the tile once; the first left_count entries are the occupied blocks. `left_count`: at most 4 occupied blocks in a tile; some tile has exactly 4 in every draw. `right_blocks`: each tile's entries name every block number of the tile once; the first right_count entries are the occupied blocks. `right_count`: at most 4 occupied blocks in a tile; some tile has exactly 4 in every draw.
All inputs are finite; a program needn't handle non-finite values.
Results may differ from the reference program's by a relative error of at most 0.0003.
Values may be sent and summed in bfloat16 or wider, within the bound.
A program may use at most 64 MiB of HBM per device.

```python
import jax
import jax.numpy as jnp
from jax import lax

BW = 256
RB = 2
KB = 5
CB = 3
CAP = 4
STEPS = 4
GRID_ROWS = 4
GRID_COLS = 4
NBL = 10
NBR = 15
ROWS = 2048
LEFT_COLS = 5120
RIGHT_ROWS = 5120
COLS = 3072
N_ROW = 4
N_COL = 4


def count_draw(key, most):
    rolls = jax.random.randint(key, (N_ROW, N_COL), 0, 32)
    counted = jnp.where(rolls < 4, 0, jnp.where(rolls < 11, 1, jnp.where(rolls < 20, 2, jnp.where(rolls < 28, 3, most))))
    counted = jnp.minimum(counted, most)
    chosen = jax.random.randint(jax.random.fold_in(key, 7), (), 0, N_ROW * N_COL)
    flat_counts = counted.reshape(-1).at[chosen].set(most)
    return flat_counts.reshape(N_ROW, N_COL).astype(jnp.int32)


def draw_left_count(key, part):
    key = jax.random.fold_in(key, 11)
    return count_draw(key, CAP)


def draw_right_count(key, part):
    key = jax.random.fold_in(key, 23)
    return count_draw(key, CAP)


def block_levels(own_key, dims, shards, least, top_value):
    def one(axis_at, parts):
        heights = jax.random.uniform(jax.random.fold_in(jax.random.fold_in(own_key, 6), axis_at), (parts,), jnp.float32, least / len(shards), top_value / len(shards))
        return jnp.repeat(jnp.exp(heights), dims[axis_at] // parts).reshape((-1,) + (1,) * (len(dims) - axis_at - 1))

    loudness = one(*shards[0])
    for cut in shards[1:]:
        loudness = loudness * one(*cut)
    return loudness


def normal_values(stream_key, shape, spread, most, cuts=(), held_as=jnp.bfloat16):
    array = spread * jax.random.normal(stream_key, shape, jnp.float32)
    if cuts:
        array = array * block_levels(stream_key, shape, cuts, -0.22, 0.18)
    return jnp.clip(array, -most, most).astype(held_as)


def setup_inputs(seed: int = 0, part: int = 0) -> dict:
    streams_of = jax.random.split(jax.random.key(seed), 7)
    part_splits = jax.random.split(jax.random.fold_in(streams_of[6], part), 7)
    return {
        "left_tiles": normal_values(part_splits[0], (ROWS, LEFT_COLS), 1.0, 6.0, ((0, 4), (1, 4))),
        "right_tiles": normal_values(part_splits[1], (RIGHT_ROWS, COLS), BW ** -0.5, 0.375, ((0, 4), (1, 4))),
        "left_blocks": jax.vmap(lambda own: jax.random.permutation(own, NBL))(jax.random.split(part_splits[2], GRID_ROWS * GRID_COLS)).reshape((GRID_ROWS, GRID_COLS, NBL)).astype(jnp.int32),
        "left_count": draw_left_count(jax.random.fold_in(jax.random.fold_in(streams_of[6], part), 71), part),
        "right_blocks": jax.vmap(lambda own: jax.random.permutation(own, NBR))(jax.random.split(part_splits[4], GRID_ROWS * GRID_COLS)).reshape((GRID_ROWS, GRID_COLS, NBR)).astype(jnp.int32),
        "right_count": draw_right_count(jax.random.fold_in(jax.random.fold_in(streams_of[6], part), 71), part),
    }


def live_grid(tile_grid, listing, occupied, block_rows, block_cols):
    block_total = block_rows * block_cols
    slot_index = jnp.arange(listing.shape[2], dtype=jnp.int32)
    block_index = jnp.arange(block_total, dtype=jnp.int32)
    hits = (listing[:, :, :, None] == block_index[None, None, None, :]) & (slot_index[None, None, :, None] < occupied[:, :, None, None])
    keep_mask = jnp.sum(hits.astype(jnp.float32), axis=2)
    keep_mask = keep_mask.reshape(N_ROW, N_COL, block_rows, block_cols).transpose(0, 2, 1, 3)
    shaped = tile_grid.reshape(N_ROW, block_rows, BW, N_COL, block_cols, BW)
    shaped = shaped * keep_mask[:, :, None, :, :, None].astype(tile_grid.dtype)
    return shaped.transpose(0, 3, 1, 2, 4, 5).reshape(N_ROW, N_COL, block_rows * BW, block_cols * BW)


def reference(left_tiles, right_tiles, left_blocks, left_count, right_blocks, right_count):
    left_live = live_grid(left_tiles, left_blocks, left_count, RB, KB)
    right_live = live_grid(right_tiles, right_blocks, right_count, KB, CB)

    def grid_row(row_index):
        here_left = lax.dynamic_index_in_dim(left_live, row_index, 0, keepdims=False).astype(jnp.float32)
        total = jnp.zeros((N_COL, RB * BW, CB * BW), jnp.float32)
        for step in range(STEPS):
            moved_left = jnp.roll(here_left, -step, axis=0)
            other_index = ((row_index + step) % N_ROW).astype(jnp.int32)
            other_right = lax.dynamic_index_in_dim(right_live, other_index, 0, keepdims=False).astype(jnp.float32)
            total = total + jnp.einsum("jab,jbc->jac", moved_left, other_right, precision=lax.Precision.HIGHEST)
        return total

    tile_out = lax.map(grid_row, jnp.arange(N_ROW, dtype=jnp.int32))
    return tile_out.transpose(0, 2, 1, 3).reshape(N_ROW * RB * BW, N_COL * CB * BW)
```

```python
import functools

import jax
import jax.numpy as jnp
from jax import lax
from jax.experimental import pallas as pl
from jax.experimental.pallas import tpu as pltpu
from jax.sharding import PartitionSpec as P

BW = 256
CAP = 4
STEPS = 4
MESH = pl.DeviceIdType.MESH


def passed_along(block, axis, distance):
    devices = range(lax.axis_size(axis))
    route = [((i - distance) % len(devices), i) for i in devices]
    return lax.ppermute(block, axis, route)


def masked(tile, listing, occupied, block_rows, block_cols):
    slot_total = listing.shape[2]
    block_index = jnp.arange(block_rows * block_cols, dtype=jnp.int32)
    slot_index = jnp.arange(slot_total, dtype=jnp.int32)
    hits = (listing[0, 0, :, None] == block_index[None, :]) & (slot_index[:, None] < occupied[0, 0])
    keep_mask = jnp.sum(hits.astype(jnp.float32), axis=0).astype(tile.dtype)
    shaped = tile.reshape(block_rows, BW, block_cols, BW) * keep_mask.reshape(
        block_rows, 1, block_cols, 1
    )
    return shaped.reshape(tile.shape)


def shifted_steps(left_tiles, right_tiles, left_blocks, left_count, right_blocks, right_count):
    left_rows = left_tiles.shape[0] // BW
    inner_blocks = left_tiles.shape[1] // BW
    right_cols = right_tiles.shape[1] // BW
    total = jnp.zeros((left_tiles.shape[0], right_tiles.shape[1]), jnp.float32)
    held_left = (left_tiles, left_blocks, left_count)
    held_right = (right_tiles, right_blocks, right_count)
    for step in range(STEPS):
        total = total + jnp.dot(
            masked(held_left[0], held_left[1], held_left[2], left_rows, inner_blocks),
            masked(held_right[0], held_right[1], held_right[2], inner_blocks, right_cols),
            preferred_element_type=jnp.float32,
        )
        if step + 1 < STEPS:
            held_left = passed_along(held_left, "col", -1)
            held_right = passed_along(held_right, "row", -1)
    return total


K_AT, C_AT = 16, 20


def kernel(
    left_ref, right_ref, left_blocks, left_count, right_blocks, right_count, out_ref,
    left_full, right_full, left_own, left_held, right_held, total, note,
    notes_row, notes_col, read_row, read_col,
    right_load, left_load, out_sem, note_sem, right_send, right_recv, left_send, left_recv, notes_send, notes_recv,
):
    z, j = lax.axis_index("row"), lax.axis_index("col")
    kb = left_ref.shape[1] // BW
    rb = left_ref.shape[0] // BW
    cb = right_ref.shape[1] // BW
    sibling = j + 1 - 2 * lax.rem(j, 2)
    partner = lax.rem(j + 2, 4)
    far = lax.rem(sibling + 2, 4)

    right_loads = [
        pltpu.make_async_copy(
            right_ref.at[pl.ds(b // cb * BW, BW), pl.ds(b % cb * BW, BW)], right_full.at[b], right_load.at[b]
        )
        for b in range(kb * cb)
    ]
    left_loads = [
        pltpu.make_async_copy(
            left_ref.at[pl.ds(b // kb * BW, BW), pl.ds(b % kb * BW, BW)], left_full.at[b], left_load.at[b]
        )
        for b in range(rb * kb)
    ]
    for load in right_loads + left_loads:
        load.start()

    barrier = pltpu.get_barrier_semaphore()
    for d in range(1, 4):
        pl.semaphore_signal(barrier, inc=1, device_id={"row": lax.rem(z + d, 4)}, device_id_type=MESH)
        pl.semaphore_signal(barrier, inc=1, device_id={"col": lax.rem(j + d, 4)}, device_id_type=MESH)

    lane = lax.broadcasted_iota(jnp.int32, note.shape, 1)
    told = jnp.full(note.shape, CAP, jnp.int32)
    for n in range(CAP):
        told = jnp.where(lane == jnp.where(n < left_count[0, 0], left_blocks[0, 0, n], -1), n, told)
        told = jnp.where(lane == K_AT + n, lax.div(right_blocks[0, 0, n], cb), told)
        column = jnp.where(n < right_count[0, 0], lax.rem(right_blocks[0, 0, n], cb), cb)
        told = jnp.where(lane == C_AT + n, column, told)
    note[...] = told
    notes_row[z] = told
    notes_col[j] = told

    empty = jnp.zeros((BW, BW), jnp.bfloat16)
    left_own[CAP] = empty
    for t in range(4):
        left_held[t, CAP] = empty

    def send_right(t, b, up):
        return pltpu.make_async_remote_copy(
            src_ref=right_held.at[t, b], dst_ref=right_held.at[t, b],
            send_sem=right_send.at[up, t, b], recv_sem=right_recv.at[t, b],
            device_id={"row": lax.rem(z + (1 if up else 3), 4)}, device_id_type=MESH,
        )

    def send_left(b, to):
        return pltpu.make_async_remote_copy(
            src_ref=left_own.at[b], dst_ref=left_held.at[j, b],
            send_sem=left_send.at[0 if to is partner else 1, b], recv_sem=left_recv.at[j, b],
            device_id={"col": to}, device_id_type=MESH,
        )

    def pass_left(b):
        return pltpu.make_async_remote_copy(
            src_ref=left_held.at[partner, b], dst_ref=left_held.at[partner, b],
            send_sem=left_send.at[2, b], recv_sem=left_recv.at[partner, b],
            device_id={"col": sibling}, device_id_type=MESH,
        )

    def got_left(t, b):
        pltpu.make_async_remote_copy(
            src_ref=left_held.at[t, b], dst_ref=left_held.at[t, b],
            send_sem=left_send.at[0, b], recv_sem=left_recv.at[t, b],
            device_id={"col": sibling}, device_id_type=MESH,
        ).wait_recv()

    def send_note(d, axis):
        own = z if axis == 0 else j
        held = notes_row if axis == 0 else notes_col
        return pltpu.make_async_remote_copy(
            src_ref=note, dst_ref=held.at[own],
            send_sem=notes_send.at[axis, d], recv_sem=notes_recv.at[axis, own],
            device_id={"row" if axis == 0 else "col": lax.rem(own + d, 4)}, device_id_type=MESH,
        )

    def got_note(d, axis):
        own = z if axis == 0 else j
        held = notes_row if axis == 0 else notes_col
        t = lax.rem(own + d, 4)
        pltpu.make_async_remote_copy(
            src_ref=note, dst_ref=held.at[t],
            send_sem=notes_send.at[axis, d], recv_sem=notes_recv.at[axis, t],
            device_id={"row" if axis == 0 else "col": t}, device_id_type=MESH,
        ).wait_recv()

    pl.semaphore_wait(barrier, 6)

    for load in right_loads:
        load.wait()
    for n in range(CAP):
        right_held[z, n] = right_full[right_blocks[0, 0, n]]

        @pl.when(z < 3)
        def _():
            send_right(z, n, 1).start()

        @pl.when(z > 0)
        def _():
            send_right(z, n, 0).start()

    for load in left_loads:
        load.wait()
    for n in range(CAP):
        left_own[n] = left_full[left_blocks[0, 0, n]]
        send_left(n, partner).start()
        send_left(n, sibling).start()

    for axis in range(2):
        for d in range(1, 4):
            send_note(d, axis).start()

    total[...] = jnp.zeros_like(total)

    for axis in range(2):
        for d in range(1, 4):
            got_note(d, axis)
    reads = (
        pltpu.make_async_copy(notes_row, read_row, note_sem.at[0]),
        pltpu.make_async_copy(notes_col, read_col, note_sem.at[1]),
    )
    for read in reads:
        read.start()
    for read in reads:
        read.wait()

    def add(t, b, own):
        k, c = read_row[t, 0, K_AT + b], read_row[t, 0, C_AT + b]
        l = j if own else lax.rem(j + t - z + 4, 4)
        block = right_held[t, b]
        for r in range(rb):
            slot = read_col[l, 0, r * kb + k]
            met = left_own[slot] if own else left_held[l, slot]
            product = jnp.dot(met, block, preferred_element_type=jnp.float32)
            for at in range(cb):
                place = (pl.ds(r * BW, BW), pl.ds(at * BW, BW))
                total[place] += jnp.where(c == at, product, 0.0)

    def take_right(d, b):
        @pl.when(z >= d)
        def _():
            send_right(z - d, b, 0).wait_recv()
            if d < 3:

                @pl.when(z < 3)
                def _():
                    send_right(z - d, b, 1).start()

        @pl.when(z + d < 4)
        def _():
            send_right(z + d, b, 0).wait_recv()
            if d < 3:

                @pl.when(z > 0)
                def _():
                    send_right(z + d, b, 0).start()

    def first(b, carry):
        take_right(1, b)
        got_left(partner, b)
        pass_left(b).start()
        add(z, b, True)
        return carry

    lax.fori_loop(0, CAP, first, 0)

    def rest_of_left(b, carry):
        got_left(sibling, b)
        got_left(far, b)
        return carry

    lax.fori_loop(0, CAP, rest_of_left, 0)

    def second(b, carry):
        take_right(2, b)

        @pl.when(z > 0)
        def _():
            add(z - 1, b, False)

        @pl.when(z < 3)
        def _():
            add(z + 1, b, False)

        return carry

    lax.fori_loop(0, CAP, second, 0)

    def third(b, carry):
        add(lax.rem(z + 2, 4), b, False)
        take_right(3, b)

        @pl.when((z == 0) | (z == 3))
        def _():
            add(3 - z, b, False)

        return carry

    lax.fori_loop(0, CAP, third, 0)

    out = pltpu.make_async_copy(total, out_ref, out_sem.at[0])
    out.start()

    def sent(b, carry):
        send_left(b, partner).wait_send()
        send_left(b, sibling).wait_send()
        pass_left(b).wait_send()
        for d in range(3):

            @pl.when((z >= d) & (z < 3))
            def _():
                send_right(z - d, b, 1).wait_send()

            @pl.when((z + d < 4) & (z > 0))
            def _():
                send_right(z + d, b, 0).wait_send()

        return carry

    lax.fori_loop(0, CAP, sent, 0)
    for axis in range(2):
        for d in range(1, 4):
            send_note(d, axis).wait_send()
    out.wait()


def packed_lines(left_tiles, right_tiles, left_blocks, left_count, right_blocks, right_count):
    rows, cols = left_tiles.shape[0], right_tiles.shape[1]
    left_total, right_total = left_tiles.size // BW**2, right_tiles.size // BW**2
    any_space = pl.BlockSpec(memory_space=pl.ANY)
    scalars = pl.BlockSpec(memory_space=pltpu.SMEM)
    dma = pltpu.SemaphoreType.DMA
    return pl.pallas_call(
        kernel,
        out_shape=jax.ShapeDtypeStruct((rows, cols), jnp.float32),
        in_specs=[any_space] * 2 + [scalars] * 4,
        out_specs=any_space,
        scratch_shapes=[
            pltpu.VMEM((left_total, BW, BW), jnp.bfloat16),
            pltpu.VMEM((right_total, BW, BW), jnp.bfloat16),
            pltpu.VMEM((CAP + 1, BW, BW), jnp.bfloat16),
            pltpu.VMEM((4, CAP + 1, BW, BW), jnp.bfloat16),
            pltpu.VMEM((4, CAP, BW, BW), jnp.bfloat16),
            pltpu.VMEM((rows, cols), jnp.float32),
            pltpu.VMEM((8, 128), jnp.int32),
            pltpu.VMEM((4, 8, 128), jnp.int32),
            pltpu.VMEM((4, 8, 128), jnp.int32),
            pltpu.SMEM((4, 8, 128), jnp.int32),
            pltpu.SMEM((4, 8, 128), jnp.int32),
            dma((right_total,)),
            dma((left_total,)),
            dma((1,)),
            dma((2,)),
            dma((2, 4, CAP)),
            dma((4, CAP)),
            dma((3, CAP)),
            dma((4, CAP)),
            dma((2, 4)),
            dma((2, 4)),
        ],
        compiler_params=pltpu.CompilerParams(
            collective_id=0, has_side_effects=True, vmem_limit_bytes=56 * 1024 * 1024
        ),
        cost_estimate=pl.CostEstimate(
            flops=2 * STEPS * 2 * CAP * BW**3, bytes_accessed=5 * 1024 * 1024, transcendentals=0
        ),
    )(left_tiles, right_tiles, left_blocks, left_count, right_blocks, right_count)


def solution(mesh):
    placed = (
        P(("groups", "row"), "col"),
        P(("groups", "row"), "col"),
        P(("groups", "row"), "col", None),
        P(("groups", "row"), "col"),
        P(("groups", "row"), "col", None),
        P(("groups", "row"), "col"),
    )
    grid = mesh.shape["row"] == 4 and mesh.shape["col"] == 4
    return jax.shard_map(
        packed_lines if grid else shifted_steps,
        mesh=mesh,
        in_specs=placed,
        out_specs=P(("groups", "row"), "col"),
        check_vma=False,
    )
```

```python
import functools

import jax
import jax.numpy as jnp
from jax import lax
from jax.experimental import pallas as pl
from jax.experimental.pallas import tpu as pltpu
from jax.sharding import PartitionSpec as P

BW = 256
CAP = 4
AHEAD = 4
STEPS = 4
MESH = pl.DeviceIdType.MESH


def passed_along(block, axis, distance):
    devices = range(lax.axis_size(axis))
    route = [((i - distance) % len(devices), i) for i in devices]
    return lax.ppermute(block, axis, route)


def masked(tile, listing, occupied, block_rows, block_cols):
    slot_total = listing.shape[2]
    block_index = jnp.arange(block_rows * block_cols, dtype=jnp.int32)
    slot_index = jnp.arange(slot_total, dtype=jnp.int32)
    hits = (listing[0, 0, :, None] == block_index[None, :]) & (slot_index[:, None] < occupied[0, 0])
    keep_mask = jnp.sum(hits.astype(jnp.float32), axis=0).astype(tile.dtype)
    shaped = tile.reshape(block_rows, BW, block_cols, BW) * keep_mask.reshape(
        block_rows, 1, block_cols, 1
    )
    return shaped.reshape(tile.shape)


def shifted_steps(left_tiles, right_tiles, left_blocks, left_count, right_blocks, right_count):
    left_rows = left_tiles.shape[0] // BW
    inner_blocks = left_tiles.shape[1] // BW
    right_cols = right_tiles.shape[1] // BW
    total = jnp.zeros((left_tiles.shape[0], right_tiles.shape[1]), jnp.float32)
    held_left = (left_tiles, left_blocks, left_count)
    held_right = (right_tiles, right_blocks, right_count)
    for step in range(STEPS):
        total = total + jnp.dot(
            masked(held_left[0], held_left[1], held_left[2], left_rows, inner_blocks),
            masked(held_right[0], held_right[1], held_right[2], inner_blocks, right_cols),
            preferred_element_type=jnp.float32,
        )
        if step + 1 < STEPS:
            held_left = passed_along(held_left, "col", -1)
            held_right = passed_along(held_right, "row", -1)
    return total


K_AT, C_AT = 16, 20


def kernel(
    left_ref, right_ref, left_blocks, left_count, right_blocks, right_count, total,
    left_full, right_full, left_own, left_held, right_held, note,
    notes_row, notes_col, read_own, read_row, read_col,
    right_load, left_load, note_sem, right_send, right_recv, left_send, left_recv, notes_send, notes_recv,
):
    z, j = lax.axis_index("row"), lax.axis_index("col")
    kb = left_ref.shape[1] // BW
    rb = left_ref.shape[0] // BW
    cb = right_ref.shape[1] // BW
    sibling = j + 1 - 2 * lax.rem(j, 2)
    partner = lax.rem(j + 2, 4)
    far = lax.rem(sibling + 2, 4)

    right_loads = [
        pltpu.make_async_copy(
            right_ref.at[pl.ds(b // cb * BW, BW), pl.ds(b % cb * BW, BW)], right_full.at[b], right_load.at[b]
        )
        for b in range(kb * cb)
    ]
    left_loads = [
        pltpu.make_async_copy(
            left_ref.at[pl.ds(b // kb * BW, BW), pl.ds(b % kb * BW, BW)], left_full.at[b], left_load.at[b]
        )
        for b in range(rb * kb)
    ]
    for load in right_loads + left_loads:
        load.start()

    barrier = pltpu.get_barrier_semaphore()
    for d in range(1, 4):
        pl.semaphore_signal(barrier, inc=1, device_id={"row": lax.rem(z + d, 4)}, device_id_type=MESH)
        pl.semaphore_signal(barrier, inc=1, device_id={"col": lax.rem(j + d, 4)}, device_id_type=MESH)

    lane = lax.broadcasted_iota(jnp.int32, note.shape, 1)
    told = jnp.full(note.shape, CAP, jnp.int32)
    for n in range(CAP):
        told = jnp.where(lane == jnp.where(n < left_count[0, 0], left_blocks[0, 0, n], -1), n, told)
        told = jnp.where(lane == K_AT + n, lax.div(right_blocks[0, 0, n], cb), told)
        column = jnp.where(n < right_count[0, 0], lax.rem(right_blocks[0, 0, n], cb), cb)
        told = jnp.where(lane == C_AT + n, column, told)
    note[...] = told
    notes_row[z] = told
    notes_col[j] = told
    own_read = pltpu.make_async_copy(note, read_own, note_sem.at[2])
    own_read.start()

    empty = jnp.zeros((BW, BW), jnp.bfloat16)
    left_own[CAP] = empty
    for t in range(4):
        left_held[t, CAP] = empty

    def send_right(t, b, up):
        return pltpu.make_async_remote_copy(
            src_ref=right_held.at[t, b], dst_ref=right_held.at[t, b],
            send_sem=right_send.at[up, t, b], recv_sem=right_recv.at[t, b],
            device_id={"row": lax.rem(z + (1 if up else 3), 4)}, device_id_type=MESH,
        )

    def send_own(b):
        @pl.when(z < 3)
        def _():
            send_right(z, b, 1).start()

        @pl.when(z > 0)
        def _():
            send_right(z, b, 0).start()

    def send_left(b, to):
        return pltpu.make_async_remote_copy(
            src_ref=left_own.at[b], dst_ref=left_held.at[j, b],
            send_sem=left_send.at[0 if to is partner else 1, b], recv_sem=left_recv.at[j, b],
            device_id={"col": to}, device_id_type=MESH,
        )

    def pass_left(b):
        return pltpu.make_async_remote_copy(
            src_ref=left_held.at[partner, b], dst_ref=left_held.at[partner, b],
            send_sem=left_send.at[2, b], recv_sem=left_recv.at[partner, b],
            device_id={"col": sibling}, device_id_type=MESH,
        )

    def got_left(t, b):
        pltpu.make_async_remote_copy(
            src_ref=left_held.at[t, b], dst_ref=left_held.at[t, b],
            send_sem=left_send.at[0, b], recv_sem=left_recv.at[t, b],
            device_id={"col": sibling}, device_id_type=MESH,
        ).wait_recv()

    def send_note(d, axis):
        own = z if axis == 0 else j
        held = notes_row if axis == 0 else notes_col
        return pltpu.make_async_remote_copy(
            src_ref=note, dst_ref=held.at[own],
            send_sem=notes_send.at[axis, d], recv_sem=notes_recv.at[axis, own],
            device_id={"row" if axis == 0 else "col": lax.rem(own + d, 4)}, device_id_type=MESH,
        )

    def got_note(d, axis):
        own = z if axis == 0 else j
        held = notes_row if axis == 0 else notes_col
        t = lax.rem(own + d, 4)
        pltpu.make_async_remote_copy(
            src_ref=note, dst_ref=held.at[t],
            send_sem=notes_send.at[axis, d], recv_sem=notes_recv.at[axis, t],
            device_id={"row" if axis == 0 else "col": t}, device_id_type=MESH,
        ).wait_recv()

    pl.semaphore_wait(barrier, 6)
    for axis in range(2):
        for d in range(1, 4):
            send_note(d, axis).start()

    for load in right_loads:
        load.wait()
    for n in range(CAP):
        right_held[z, n] = right_full[right_blocks[0, 0, n]]
        if n < AHEAD:
            send_own(n)

    for load in left_loads:
        load.wait()
    for n in range(CAP):
        left_own[n] = left_full[left_blocks[0, 0, n]]
        send_left(n, partner).start()
        send_left(n, sibling).start()

    total[...] = jnp.zeros_like(total)

    own_read.wait()

    def add(t, b, own):
        l = lax.rem(j + t - z + 4, 4)
        k = read_own[0, K_AT + b] if own else read_row[t, 0, K_AT + b]
        c = read_own[0, C_AT + b] if own else read_row[t, 0, C_AT + b]
        block = right_held[t, b]
        for r in range(rb):
            slot = read_own[0, r * kb + k] if own else read_col[l, 0, r * kb + k]
            met = left_own[slot] if own else left_held[l, slot]
            product = jnp.dot(met, block, preferred_element_type=jnp.float32)
            for at in range(cb):
                place = (pl.ds(r * BW, BW), pl.ds(at * BW, BW))
                total[place] += jnp.where(c == at, product, 0.0)

    def take_right(d, b):
        @pl.when(z >= d)
        def _():
            send_right(z - d, b, 0).wait_recv()
            if d < 3:

                @pl.when(z < 3)
                def _():
                    send_right(z - d, b, 1).start()

        @pl.when(z + d < 4)
        def _():
            send_right(z + d, b, 0).wait_recv()
            if d < 3:

                @pl.when(z > 0)
                def _():
                    send_right(z + d, b, 0).start()

    def first(b, carry):
        take_right(1, b)

        @pl.when(b + AHEAD < CAP)
        def _():
            send_own(b + AHEAD)

        got_left(partner, b)
        pass_left(b).start()
        add(z, b, True)
        return carry

    lax.fori_loop(0, CAP, first, 0)

    def rest_of_left(b, carry):
        got_left(sibling, b)
        got_left(far, b)
        return carry

    lax.fori_loop(0, CAP, rest_of_left, 0)
    for axis in range(2):
        for d in range(1, 4):
            got_note(d, axis)
    reads = (
        pltpu.make_async_copy(notes_row, read_row, note_sem.at[0]),
        pltpu.make_async_copy(notes_col, read_col, note_sem.at[1]),
    )
    for read in reads:
        read.start()
    for read in reads:
        read.wait()

    def second(b, carry):
        take_right(2, b)

        @pl.when(z > 0)
        def _():
            add(z - 1, b, False)

        @pl.when(z < 3)
        def _():
            add(z + 1, b, False)

        return carry

    lax.fori_loop(0, CAP, second, 0)

    def third(b, carry):
        add(lax.rem(z + 2, 4), b, False)
        take_right(3, b)

        @pl.when((z == 0) | (z == 3))
        def _():
            add(3 - z, b, False)

        return carry

    lax.fori_loop(0, CAP, third, 0)

    def sent(b, carry):
        send_left(b, partner).wait_send()
        send_left(b, sibling).wait_send()
        pass_left(b).wait_send()
        for d in range(3):

            @pl.when((z >= d) & (z < 3))
            def _():
                send_right(z - d, b, 1).wait_send()

            @pl.when((z + d < 4) & (z > 0))
            def _():
                send_right(z + d, b, 0).wait_send()

        return carry

    lax.fori_loop(0, CAP, sent, 0)
    for axis in range(2):
        for d in range(1, 4):
            send_note(d, axis).wait_send()


def packed_lines(left_tiles, right_tiles, left_blocks, left_count, right_blocks, right_count):
    rows, cols = left_tiles.shape[0], right_tiles.shape[1]
    left_total, right_total = left_tiles.size // BW**2, right_tiles.size // BW**2
    any_space = pl.BlockSpec(memory_space=pl.ANY)
    scalars = pl.BlockSpec(memory_space=pltpu.SMEM)
    dma = pltpu.SemaphoreType.DMA
    return pl.pallas_call(
        kernel,
        out_shape=pltpu.VMEM((rows, cols), jnp.float32),
        in_specs=[any_space] * 2 + [scalars] * 4,
        out_specs=pl.BlockSpec(memory_space=pltpu.VMEM),
        scratch_shapes=[
            pltpu.VMEM((left_total, BW, BW), jnp.bfloat16),
            pltpu.VMEM((right_total, BW, BW), jnp.bfloat16),
            pltpu.VMEM((CAP + 1, BW, BW), jnp.bfloat16),
            pltpu.VMEM((4, CAP + 1, BW, BW), jnp.bfloat16),
            pltpu.VMEM((4, CAP, BW, BW), jnp.bfloat16),
            pltpu.VMEM((8, 128), jnp.int32),
            pltpu.VMEM((4, 8, 128), jnp.int32),
            pltpu.VMEM((4, 8, 128), jnp.int32),
            pltpu.SMEM((8, 128), jnp.int32),
            pltpu.SMEM((4, 8, 128), jnp.int32),
            pltpu.SMEM((4, 8, 128), jnp.int32),
            dma((right_total,)),
            dma((left_total,)),
            dma((3,)),
            dma((2, 4, CAP)),
            dma((4, CAP)),
            dma((3, CAP)),
            dma((4, CAP)),
            dma((2, 4)),
            dma((2, 4)),
        ],
        compiler_params=pltpu.CompilerParams(
            collective_id=0, has_side_effects=True, vmem_limit_bytes=56 * 1024 * 1024
        ),
        cost_estimate=pl.CostEstimate(
            flops=2 * STEPS * 2 * CAP * BW**3, bytes_accessed=5 * 1024 * 1024, transcendentals=0
        ),
    )(left_tiles, right_tiles, left_blocks, left_count, right_blocks, right_count)


def solution(mesh):
    placed = (
        P(("groups", "row"), "col"),
        P(("groups", "row"), "col"),
        P(("groups", "row"), "col", None),
        P(("groups", "row"), "col"),
        P(("groups", "row"), "col", None),
        P(("groups", "row"), "col"),
    )
    grid = mesh.shape["row"] == 4 and mesh.shape["col"] == 4
    return jax.shard_map(
        packed_lines if grid else shifted_steps,
        mesh=mesh,
        in_specs=placed,
        out_specs=P(("groups", "row"), "col"),
        check_vma=False,
    )
```

```python
import functools

import jax
import jax.numpy as jnp
from jax import lax
from jax.experimental import pallas as pl
from jax.experimental.pallas import tpu as pltpu
from jax.sharding import PartitionSpec as P

BW = 256
CAP = 4
STEPS = 4
MESH = pl.DeviceIdType.MESH


def passed_along(block, axis, distance):
    devices = range(lax.axis_size(axis))
    route = [((i - distance) % len(devices), i) for i in devices]
    return lax.ppermute(block, axis, route)


def masked(tile, listing, occupied, block_rows, block_cols):
    slot_total = listing.shape[2]
    block_index = jnp.arange(block_rows * block_cols, dtype=jnp.int32)
    slot_index = jnp.arange(slot_total, dtype=jnp.int32)
    hits = (listing[0, 0, :, None] == block_index[None, :]) & (slot_index[:, None] < occupied[0, 0])
    keep_mask = jnp.sum(hits.astype(jnp.float32), axis=0).astype(tile.dtype)
    shaped = tile.reshape(block_rows, BW, block_cols, BW) * keep_mask.reshape(
        block_rows, 1, block_cols, 1
    )
    return shaped.reshape(tile.shape)


def shifted_steps(left_tiles, right_tiles, left_blocks, left_count, right_blocks, right_count):
    left_rows = left_tiles.shape[0] // BW
    inner_blocks = left_tiles.shape[1] // BW
    right_cols = right_tiles.shape[1] // BW
    total = jnp.zeros((left_tiles.shape[0], right_tiles.shape[1]), jnp.float32)
    held_left = (left_tiles, left_blocks, left_count)
    held_right = (right_tiles, right_blocks, right_count)
    for step in range(STEPS):
        total = total + jnp.dot(
            masked(held_left[0], held_left[1], held_left[2], left_rows, inner_blocks),
            masked(held_right[0], held_right[1], held_right[2], inner_blocks, right_cols),
            preferred_element_type=jnp.float32,
        )
        if step + 1 < STEPS:
            held_left = passed_along(held_left, "col", -1)
            held_right = passed_along(held_right, "row", -1)
    return total


K_AT, C_AT = 16, 20


def kernel(
    left_ref, right_ref, left_blocks, left_count, right_blocks, right_count, total,
    left_full, right_full, left_own, left_held, right_held, note,
    notes_row, notes_col, read_own, read_row, read_col,
    right_load, left_load, note_sem, right_send, right_recv, left_send, left_recv, row_notes_send, row_notes_recv, notes_send, notes_recv,
):
    z, j = lax.axis_index("row"), lax.axis_index("col")
    kb = left_ref.shape[1] // BW
    rb = left_ref.shape[0] // BW
    cb = right_ref.shape[1] // BW
    sibling = j + 1 - 2 * lax.rem(j, 2)
    partner = lax.rem(j + 2, 4)
    far = lax.rem(sibling + 2, 4)

    right_loads = [
        pltpu.make_async_copy(
            right_ref.at[pl.ds(b // cb * BW, BW), pl.ds(b % cb * BW, BW)], right_full.at[b], right_load.at[b]
        )
        for b in range(kb * cb)
    ]
    left_loads = [
        pltpu.make_async_copy(
            left_ref.at[pl.ds(b // kb * BW, BW), pl.ds(b % kb * BW, BW)], left_full.at[b], left_load.at[b]
        )
        for b in range(rb * kb)
    ]
    for load in right_loads + left_loads:
        load.start()

    barrier = pltpu.get_barrier_semaphore()
    for d in range(1, 4):
        pl.semaphore_signal(barrier, inc=1, device_id={"col": lax.rem(j + d, 4)}, device_id_type=MESH)

    lane = lax.broadcasted_iota(jnp.int32, note.shape, 1)
    told = jnp.full(note.shape, CAP, jnp.int32)
    for n in range(CAP):
        told = jnp.where(lane == jnp.where(n < left_count[0, 0], left_blocks[0, 0, n], -1), n, told)
        told = jnp.where(lane == K_AT + n, lax.div(right_blocks[0, 0, n], cb), told)
        column = jnp.where(n < right_count[0, 0], lax.rem(right_blocks[0, 0, n], cb), cb)
        told = jnp.where(lane == C_AT + n, column, told)
    note[...] = told
    notes_row[z] = told
    notes_col[j] = told
    own_read = pltpu.make_async_copy(note, read_own, note_sem.at[2])
    own_read.start()

    empty = jnp.zeros((BW, BW), jnp.bfloat16)
    left_own[CAP] = empty
    for t in range(4):
        left_held[t, CAP] = empty

    def send_right(t, b, up):
        return pltpu.make_async_remote_copy(
            src_ref=right_held.at[t, b], dst_ref=right_held.at[t, b],
            send_sem=right_send.at[up, t, b], recv_sem=right_recv.at[t, b],
            device_id={"row": lax.rem(z + (1 if up else 3), 4)}, device_id_type=MESH,
        )

    def send_left(b, to):
        return pltpu.make_async_remote_copy(
            src_ref=left_own.at[b], dst_ref=left_held.at[j, b],
            send_sem=left_send.at[0 if to is partner else 1, b], recv_sem=left_recv.at[j, b],
            device_id={"col": to}, device_id_type=MESH,
        )

    def pass_left(b):
        return pltpu.make_async_remote_copy(
            src_ref=left_held.at[partner, b], dst_ref=left_held.at[partner, b],
            send_sem=left_send.at[2, b], recv_sem=left_recv.at[partner, b],
            device_id={"col": sibling}, device_id_type=MESH,
        )

    def got_left(t, b):
        pltpu.make_async_remote_copy(
            src_ref=left_held.at[t, b], dst_ref=left_held.at[t, b],
            send_sem=left_send.at[0, b], recv_sem=left_recv.at[t, b],
            device_id={"col": sibling}, device_id_type=MESH,
        ).wait_recv()

    def send_row_note(t, up):
        return pltpu.make_async_remote_copy(
            src_ref=notes_row.at[t], dst_ref=notes_row.at[t],
            send_sem=row_notes_send.at[up, t], recv_sem=row_notes_recv.at[t],
            device_id={"row": lax.rem(z + (1 if up else 3), 4)}, device_id_type=MESH,
        )

    def send_note(d):
        return pltpu.make_async_remote_copy(
            src_ref=note, dst_ref=notes_col.at[j],
            send_sem=notes_send.at[d], recv_sem=notes_recv.at[j],
            device_id={"col": lax.rem(j + d, 4)}, device_id_type=MESH,
        )

    def got_note(d):
        t = lax.rem(j + d, 4)
        pltpu.make_async_remote_copy(
            src_ref=note, dst_ref=notes_col.at[t],
            send_sem=notes_send.at[d], recv_sem=notes_recv.at[t],
            device_id={"col": t}, device_id_type=MESH,
        ).wait_recv()

    pl.semaphore_wait(barrier, 3 + jnp.minimum(z, 1))

    @pl.when(z > 0)
    def _():
        pl.semaphore_signal(barrier, inc=1, device_id={"row": z - 1}, device_id_type=MESH)
        send_row_note(z, 0).start()

    @pl.when(z < 3)
    def _():
        pl.semaphore_signal(barrier, inc=1, device_id={"row": z + 1}, device_id_type=MESH)

    for d in range(1, 4):
        send_note(d).start()

    for load in right_loads:
        load.wait()
    for n in range(CAP):
        right_held[z, n] = right_full[right_blocks[0, 0, n]]

        @pl.when(z > 0)
        def _():
            send_right(z, n, 0).start()

    @pl.when(z < 3)
    def _():
        pl.semaphore_wait(barrier, 1)
        send_row_note(z, 1).start()
        for n in range(CAP):
            send_right(z, n, 1).start()

    for load in left_loads:
        load.wait()
    for n in range(CAP):
        left_own[n] = left_full[left_blocks[0, 0, n]]
        send_left(n, partner).start()
        send_left(n, sibling).start()

    total[...] = jnp.zeros_like(total)

    own_read.wait()

    def add(t, b, own):
        l = lax.rem(j + t - z + 4, 4)
        k = read_own[0, K_AT + b] if own else read_row[t, 0, K_AT + b]
        c = read_own[0, C_AT + b] if own else read_row[t, 0, C_AT + b]
        block = right_held[t, b]
        for r in range(rb):
            slot = read_own[0, r * kb + k] if own else read_col[l, 0, r * kb + k]
            met = left_own[slot] if own else left_held[l, slot]
            product = jnp.dot(met, block, preferred_element_type=jnp.float32)
            for at in range(cb):
                place = (pl.ds(r * BW, BW), pl.ds(at * BW, BW))
                total[place] += jnp.where(c == at, product, 0.0)

    def take_right(d, b):
        @pl.when(z >= d)
        def _():
            send_right(z - d, b, 0).wait_recv()
            if d < 3:

                @pl.when(z < 3)
                def _():
                    send_right(z - d, b, 1).start()

        @pl.when(z + d < 4)
        def _():
            send_right(z + d, b, 0).wait_recv()
            if d < 3:

                @pl.when(z > 0)
                def _():
                    send_right(z + d, b, 0).start()

    def take_note(d):
        for up in (1, 0):
            t = z - d if up else z + d

            @pl.when((z >= d) if up else (z + d < 4))
            def _():
                send_row_note(t, up).wait_recv()
                if d < 3:

                    @pl.when((z < 3) if up else (z > 0))
                    def _():
                        send_row_note(t, up).start()

                read = pltpu.make_async_copy(notes_row.at[t], read_row.at[t], note_sem.at[0])
                read.start()
                read.wait()

    take_note(1)

    def first(b, carry):
        take_right(1, b)

        got_left(partner, b)
        pass_left(b).start()
        add(z, b, True)
        return carry

    lax.fori_loop(0, CAP, first, 0)

    def rest_of_left(b, carry):
        got_left(sibling, b)
        got_left(far, b)
        return carry

    lax.fori_loop(0, CAP, rest_of_left, 0)
    for d in range(1, 4):
        got_note(d)
    read = pltpu.make_async_copy(notes_col, read_col, note_sem.at[1])
    read.start()
    read.wait()
    take_note(2)

    def second(b, carry):
        take_right(2, b)

        @pl.when(z > 0)
        def _():
            add(z - 1, b, False)

        @pl.when(z < 3)
        def _():
            add(z + 1, b, False)

        return carry

    lax.fori_loop(0, CAP, second, 0)

    def third(b, carry):
        add(lax.rem(z + 2, 4), b, False)
        take_right(3, b)

        @pl.when((z == 0) | (z == 3))
        def _():
            add(3 - z, b, False)

        return carry

    take_note(3)
    lax.fori_loop(0, CAP, third, 0)

    def sent(b, carry):
        send_left(b, partner).wait_send()
        send_left(b, sibling).wait_send()
        pass_left(b).wait_send()
        for d in range(3):

            @pl.when((z >= d) & (z < 3))
            def _():
                send_right(z - d, b, 1).wait_send()

            @pl.when((z + d < 4) & (z > 0))
            def _():
                send_right(z + d, b, 0).wait_send()

        return carry

    lax.fori_loop(0, CAP, sent, 0)
    for d in range(1, 4):
        send_note(d).wait_send()
    for d in range(3):

        @pl.when((z >= d) & (z < 3))
        def _():
            send_row_note(z - d, 1).wait_send()

        @pl.when((z + d < 4) & (z > 0))
        def _():
            send_row_note(z + d, 0).wait_send()


def packed_lines(left_tiles, right_tiles, left_blocks, left_count, right_blocks, right_count):
    rows, cols = left_tiles.shape[0], right_tiles.shape[1]
    left_total, right_total = left_tiles.size // BW**2, right_tiles.size // BW**2
    any_space = pl.BlockSpec(memory_space=pl.ANY)
    scalars = pl.BlockSpec(memory_space=pltpu.SMEM)
    dma = pltpu.SemaphoreType.DMA
    return pl.pallas_call(
        kernel,
        out_shape=pltpu.VMEM((rows, cols), jnp.float32),
        in_specs=[any_space] * 2 + [scalars] * 4,
        out_specs=pl.BlockSpec(memory_space=pltpu.VMEM),
        scratch_shapes=[
            pltpu.VMEM((left_total, BW, BW), jnp.bfloat16),
            pltpu.VMEM((right_total, BW, BW), jnp.bfloat16),
            pltpu.VMEM((CAP + 1, BW, BW), jnp.bfloat16),
            pltpu.VMEM((4, CAP + 1, BW, BW), jnp.bfloat16),
            pltpu.VMEM((4, CAP, BW, BW), jnp.bfloat16),
            pltpu.VMEM((8, 128), jnp.int32),
            pltpu.VMEM((4, 8, 128), jnp.int32),
            pltpu.VMEM((4, 8, 128), jnp.int32),
            pltpu.SMEM((8, 128), jnp.int32),
            pltpu.SMEM((4, 8, 128), jnp.int32),
            pltpu.SMEM((4, 8, 128), jnp.int32),
            dma((right_total,)),
            dma((left_total,)),
            dma((3,)),
            dma((2, 4, CAP)),
            dma((4, CAP)),
            dma((3, CAP)),
            dma((4, CAP)),
            dma((2, 4)),
            dma((4,)),
            dma((4,)),
            dma((4,)),
        ],
        compiler_params=pltpu.CompilerParams(
            collective_id=0, has_side_effects=True, vmem_limit_bytes=56 * 1024 * 1024
        ),
        cost_estimate=pl.CostEstimate(
            flops=2 * STEPS * 2 * CAP * BW**3, bytes_accessed=5 * 1024 * 1024, transcendentals=0
        ),
    )(left_tiles, right_tiles, left_blocks, left_count, right_blocks, right_count)


def solution(mesh):
    placed = (
        P(("groups", "row"), "col"),
        P(("groups", "row"), "col"),
        P(("groups", "row"), "col", None),
        P(("groups", "row"), "col"),
        P(("groups", "row"), "col", None),
        P(("groups", "row"), "col"),
    )
    grid = mesh.shape["row"] == 4 and mesh.shape["col"] == 4
    return jax.shard_map(
        packed_lines if grid else shifted_steps,
        mesh=mesh,
        in_specs=placed,
        out_specs=P(("groups", "row"), "col"),
        check_vma=False,
    )
```

```python
import functools

import jax
import jax.numpy as jnp
from jax import lax
from jax.experimental import pallas as pl
from jax.experimental.pallas import tpu as pltpu
from jax.sharding import PartitionSpec as P

BW = 256
CAP = 4
AHEAD = 4
STEPS = 4
MESH = pl.DeviceIdType.MESH


def passed_along(block, axis, distance):
    devices = range(lax.axis_size(axis))
    route = [((i - distance) % len(devices), i) for i in devices]
    return lax.ppermute(block, axis, route)


def masked(tile, listing, occupied, block_rows, block_cols):
    slot_total = listing.shape[2]
    block_index = jnp.arange(block_rows * block_cols, dtype=jnp.int32)
    slot_index = jnp.arange(slot_total, dtype=jnp.int32)
    hits = (listing[0, 0, :, None] == block_index[None, :]) & (slot_index[:, None] < occupied[0, 0])
    keep_mask = jnp.sum(hits.astype(jnp.float32), axis=0).astype(tile.dtype)
    shaped = tile.reshape(block_rows, BW, block_cols, BW) * keep_mask.reshape(
        block_rows, 1, block_cols, 1
    )
    return shaped.reshape(tile.shape)


def shifted_steps(left_tiles, right_tiles, left_blocks, left_count, right_blocks, right_count):
    left_rows = left_tiles.shape[0] // BW
    inner_blocks = left_tiles.shape[1] // BW
    right_cols = right_tiles.shape[1] // BW
    total = jnp.zeros((left_tiles.shape[0], right_tiles.shape[1]), jnp.float32)
    held_left = (left_tiles, left_blocks, left_count)
    held_right = (right_tiles, right_blocks, right_count)
    for step in range(STEPS):
        total = total + jnp.dot(
            masked(held_left[0], held_left[1], held_left[2], left_rows, inner_blocks),
            masked(held_right[0], held_right[1], held_right[2], inner_blocks, right_cols),
            preferred_element_type=jnp.float32,
        )
        if step + 1 < STEPS:
            held_left = passed_along(held_left, "col", -1)
            held_right = passed_along(held_right, "row", -1)
    return total


K_AT, C_AT = 16, 20


def kernel(
    left_ref, right_ref, left_blocks, left_count, right_blocks, right_count, total,
    left_full, right_full, left_own, left_held, right_held, note,
    notes_row, notes_col, read_own, read_row, read_col,
    right_load, left_load, note_sem, right_send, right_recv, left_send, left_recv, notes_send, notes_recv,
):
    z, j = lax.axis_index("row"), lax.axis_index("col")
    kb = left_ref.shape[1] // BW
    rb = left_ref.shape[0] // BW
    cb = right_ref.shape[1] // BW
    sibling = j + 1 - 2 * lax.rem(j, 2)
    partner = lax.rem(j + 2, 4)
    far = lax.rem(sibling + 2, 4)

    right_loads = [
        pltpu.make_async_copy(
            right_ref.at[pl.ds(b // cb * BW, BW), pl.ds(b % cb * BW, BW)], right_full.at[b], right_load.at[b]
        )
        for b in range(kb * cb)
    ]
    left_loads = [
        pltpu.make_async_copy(
            left_ref.at[pl.ds(b // kb * BW, BW), pl.ds(b % kb * BW, BW)], left_full.at[b], left_load.at[b]
        )
        for b in range(rb * kb)
    ]
    for load in right_loads + left_loads:
        load.start()

    barrier = pltpu.get_barrier_semaphore()
    for d in range(1, 4):
        pl.semaphore_signal(barrier, inc=1, device_id={"row": lax.rem(z + d, 4)}, device_id_type=MESH)
        pl.semaphore_signal(barrier, inc=1, device_id={"col": lax.rem(j + d, 4)}, device_id_type=MESH)

    lane = lax.broadcasted_iota(jnp.int32, note.shape, 1)
    told = jnp.full(note.shape, CAP, jnp.int32)
    for n in range(CAP):
        told = jnp.where(lane == jnp.where(n < left_count[0, 0], left_blocks[0, 0, n], -1), n, told)
        told = jnp.where(lane == K_AT + n, lax.div(right_blocks[0, 0, n], cb), told)
        column = jnp.where(n < right_count[0, 0], lax.rem(right_blocks[0, 0, n], cb), cb)
        told = jnp.where(lane == C_AT + n, column, told)
    note[...] = told
    notes_row[z] = told
    notes_col[j] = told
    own_read = pltpu.make_async_copy(note, read_own, note_sem.at[2])
    own_read.start()

    empty = jnp.zeros((BW, BW), jnp.bfloat16)
    left_own[CAP] = empty
    for t in range(4):
        left_held[t, CAP] = empty

    def send_right(t, b, up):
        return pltpu.make_async_remote_copy(
            src_ref=right_held.at[t, b], dst_ref=right_held.at[t, b],
            send_sem=right_send.at[up, t, b], recv_sem=right_recv.at[t, b],
            device_id={"row": lax.rem(z + (1 if up else 3), 4)}, device_id_type=MESH,
        )

    def send_own(b):
        @pl.when(z < 3)
        def _():
            send_right(z, b, 1).start()

        @pl.when(z > 0)
        def _():
            send_right(z, b, 0).start()

    def send_left(b, to):
        return pltpu.make_async_remote_copy(
            src_ref=left_own.at[b], dst_ref=left_held.at[j, b],
            send_sem=left_send.at[0 if to is partner else 1, b], recv_sem=left_recv.at[j, b],
            device_id={"col": to}, device_id_type=MESH,
        )

    def pass_left(b):
        return pltpu.make_async_remote_copy(
            src_ref=left_held.at[partner, b], dst_ref=left_held.at[partner, b],
            send_sem=left_send.at[2, b], recv_sem=left_recv.at[partner, b],
            device_id={"col": sibling}, device_id_type=MESH,
        )

    def got_left(t, b):
        pltpu.make_async_remote_copy(
            src_ref=left_held.at[t, b], dst_ref=left_held.at[t, b],
            send_sem=left_send.at[0, b], recv_sem=left_recv.at[t, b],
            device_id={"col": sibling}, device_id_type=MESH,
        ).wait_recv()

    def send_note(d, axis):
        own = z if axis == 0 else j
        held = notes_row if axis == 0 else notes_col
        return pltpu.make_async_remote_copy(
            src_ref=note, dst_ref=held.at[own],
            send_sem=notes_send.at[axis, d], recv_sem=notes_recv.at[axis, own],
            device_id={"row" if axis == 0 else "col": lax.rem(own + d, 4)}, device_id_type=MESH,
        )

    def got_note(d, axis):
        own = z if axis == 0 else j
        held = notes_row if axis == 0 else notes_col
        t = lax.rem(own + d, 4)
        pltpu.make_async_remote_copy(
            src_ref=note, dst_ref=held.at[t],
            send_sem=notes_send.at[axis, d], recv_sem=notes_recv.at[axis, t],
            device_id={"row" if axis == 0 else "col": t}, device_id_type=MESH,
        ).wait_recv()

    pl.semaphore_wait(barrier, 6)
    for axis in range(2):
        for d in range(1, 4):
            send_note(d, axis).start()

    for load in right_loads:
        load.wait()
    for n in range(CAP):
        right_held[z, n] = right_full[right_blocks[0, 0, n]]
        if n < AHEAD:
            send_own(n)

    for load in left_loads:
        load.wait()
    for n in range(CAP):
        left_own[n] = left_full[left_blocks[0, 0, n]]
        send_left(n, partner).start()
        send_left(n, sibling).start()

    total[...] = jnp.zeros_like(total)

    own_read.wait()

    def add(t, b, own):
        l = lax.rem(j + t - z + 4, 4)
        k = read_own[0, K_AT + b] if own else read_row[t, 0, K_AT + b]
        c = read_own[0, C_AT + b] if own else read_row[t, 0, C_AT + b]
        block = right_held[t, b]
        for r in range(rb):
            slot = read_own[0, r * kb + k] if own else read_col[l, 0, r * kb + k]
            met = left_own[slot] if own else left_held[l, slot]
            product = jnp.dot(met, block, preferred_element_type=jnp.float32)
            for at in range(cb):
                place = (pl.ds(r * BW, BW), pl.ds(at * BW, BW))
                total[place] += jnp.where(c == at, product, 0.0)

    def take_right(d, b):
        @pl.when(z >= d)
        def _():
            send_right(z - d, b, 0).wait_recv()
            if d < 3:

                @pl.when(z < 3)
                def _():
                    send_right(z - d, b, 1).start()

        @pl.when(z + d < 4)
        def _():
            send_right(z + d, b, 0).wait_recv()
            if d < 3:

                @pl.when(z > 0)
                def _():
                    send_right(z + d, b, 0).start()

    def first(b, carry):
        take_right(1, b)

        @pl.when(b + AHEAD < CAP)
        def _():
            send_own(b + AHEAD)

        got_left(partner, b)
        pass_left(b).start()
        add(z, b, True)
        return carry

    lax.fori_loop(0, CAP, first, 0)

    def rest_of_left(b, carry):
        take_right(2, b)
        got_left(sibling, b)
        got_left(far, b)
        return carry

    lax.fori_loop(0, CAP, rest_of_left, 0)
    for axis in range(2):
        for d in range(1, 4):
            got_note(d, axis)
    reads = (
        pltpu.make_async_copy(notes_row, read_row, note_sem.at[0]),
        pltpu.make_async_copy(notes_col, read_col, note_sem.at[1]),
    )
    for read in reads:
        read.start()
    for read in reads:
        read.wait()

    def second(b, carry):
        @pl.when(z > 0)
        def _():
            add(z - 1, b, False)

        @pl.when(z < 3)
        def _():
            add(z + 1, b, False)

        return carry

    lax.fori_loop(0, CAP, second, 0)

    def third(b, carry):
        add(lax.rem(z + 2, 4), b, False)
        take_right(3, b)

        @pl.when((z == 0) | (z == 3))
        def _():
            add(3 - z, b, False)

        return carry

    lax.fori_loop(0, CAP, third, 0)

    def sent(b, carry):
        send_left(b, partner).wait_send()
        send_left(b, sibling).wait_send()
        pass_left(b).wait_send()
        for d in range(3):

            @pl.when((z >= d) & (z < 3))
            def _():
                send_right(z - d, b, 1).wait_send()

            @pl.when((z + d < 4) & (z > 0))
            def _():
                send_right(z + d, b, 0).wait_send()

        return carry

    lax.fori_loop(0, CAP, sent, 0)
    for axis in range(2):
        for d in range(1, 4):
            send_note(d, axis).wait_send()


def packed_lines(left_tiles, right_tiles, left_blocks, left_count, right_blocks, right_count):
    rows, cols = left_tiles.shape[0], right_tiles.shape[1]
    left_total, right_total = left_tiles.size // BW**2, right_tiles.size // BW**2
    any_space = pl.BlockSpec(memory_space=pl.ANY)
    scalars = pl.BlockSpec(memory_space=pltpu.SMEM)
    dma = pltpu.SemaphoreType.DMA
    return pl.pallas_call(
        kernel,
        out_shape=pltpu.VMEM((rows, cols), jnp.float32),
        in_specs=[any_space] * 2 + [scalars] * 4,
        out_specs=pl.BlockSpec(memory_space=pltpu.VMEM),
        scratch_shapes=[
            pltpu.VMEM((left_total, BW, BW), jnp.bfloat16),
            pltpu.VMEM((right_total, BW, BW), jnp.bfloat16),
            pltpu.VMEM((CAP + 1, BW, BW), jnp.bfloat16),
            pltpu.VMEM((4, CAP + 1, BW, BW), jnp.bfloat16),
            pltpu.VMEM((4, CAP, BW, BW), jnp.bfloat16),
            pltpu.VMEM((8, 128), jnp.int32),
            pltpu.VMEM((4, 8, 128), jnp.int32),
            pltpu.VMEM((4, 8, 128), jnp.int32),
            pltpu.SMEM((8, 128), jnp.int32),
            pltpu.SMEM((4, 8, 128), jnp.int32),
            pltpu.SMEM((4, 8, 128), jnp.int32),
            dma((right_total,)),
            dma((left_total,)),
            dma((3,)),
            dma((2, 4, CAP)),
            dma((4, CAP)),
            dma((3, CAP)),
            dma((4, CAP)),
            dma((2, 4)),
            dma((2, 4)),
        ],
        compiler_params=pltpu.CompilerParams(
            collective_id=0, has_side_effects=True, vmem_limit_bytes=56 * 1024 * 1024
        ),
        cost_estimate=pl.CostEstimate(
            flops=2 * STEPS * 2 * CAP * BW**3, bytes_accessed=5 * 1024 * 1024, transcendentals=0
        ),
    )(left_tiles, right_tiles, left_blocks, left_count, right_blocks, right_count)


def solution(mesh):
    placed = (
        P(("groups", "row"), "col"),
        P(("groups", "row"), "col"),
        P(("groups", "row"), "col", None),
        P(("groups", "row"), "col"),
        P(("groups", "row"), "col", None),
        P(("groups", "row"), "col"),
    )
    grid = mesh.shape["row"] == 4 and mesh.shape["col"] == 4
    return jax.shard_map(
        packed_lines if grid else shifted_steps,
        mesh=mesh,
        in_specs=placed,
        out_specs=P(("groups", "row"), "col"),
        check_vma=False,
    )
```
